256 devices in a mesh: team: 64 (over z, y_lo, x), rep: 2 (over core), feat: 2 (over y_hi).
Axes of the slice: x: 4, y: 4 (y_hi: 2, y_lo: 2; y = y_hi * 2 + y_lo), z: 8, core: 2. Of those that a mesh axis runs over, the one named last changes fastest.
Arguments:
- node_feats: bfloat16 [262144, 128], P('team'), may hold values from -6 to 6
- tile_vals: bfloat16 [1024, 2, 5, 8, 128, 128], P('team', 'feat', None, 'rep'), may hold values from -0.125 to 0.125
- tile_cols: int32 [1024, 2, 5, 8], P('team', 'feat', None, 'rep'), may hold values from 0 to 31
- tile_count: int32 [1024, 2, 5], P('team', 'feat'), may hold values from 0 to 8
- node_count: int32 [64], P('team'), may hold values from 2048 to 4096
- weight: bfloat16 [128, 256], replicated, may hold values from -0.5 to 0.5
- bias: bfloat16 [256], replicated, may hold values from -3 to 3
Outputs:
- hidden: bfloat16 [262144, 256], P(('team', 'rep'), 'feat')
The draws below stay inside these ranges and needn't reach their ends.
All inputs are finite; a program needn't handle non-finite values.
Results may differ from the reference program's by a relative error of at most 0.0044.
Values may be sent and summed in bfloat16 or wider, within the bound.
No kernel may reach another device: no remote copies, remote signals or barrier semaphores. Data moves between devices by JAX's collectives and lax.ppermute only.
A program may use at most 128 MiB of HBM per device.

```python
import jax
import jax.numpy as jnp
from jax import lax

FEAT = 128
HID = 256
TILE = 128
REACH = 2
SLOTS = 8
GRP_DEV = 16
SPAN = 5
GROUPS = 1024
SLAB = 4096
NODES = 262144
N_TEAM = 64
N_FEAT = 2


def plant(array, stream_key, smallest, high):
    place = [jax.random.randint(jax.random.fold_in(stream_key, axis), (), 0, length) for axis, length in enumerate(array.shape)]
    longest = array.shape.index(max(array.shape))
    next_to = place[:longest] + [(place[longest] + 1) % array.shape[longest]] + place[longest + 1:]
    return array.at[tuple(place)].set(smallest).at[tuple(next_to)].set(high)


def level_of(own_key, extent, cuts, least, high):
    gain = 1.0
    for axis_at, blocks in cuts:
        heights = jax.random.uniform(jax.random.fold_in(jax.random.fold_in(own_key, 6), axis_at), (blocks,), jnp.float32, least / len(cuts), high / len(cuts))
        gain = gain * jnp.repeat(jnp.exp(heights), extent[axis_at] // blocks).reshape((-1,) + (1,) * (len(extent) - 1 - axis_at))
    return gain


def gaussian(stream_key, dims, deviation, bound, cuts=(), held_as=jnp.bfloat16):
    values = jax.random.normal(stream_key, dims, jnp.float32) * deviation
    if len(cuts) > 0:
        values = level_of(stream_key, dims, cuts, -0.22, 0.18) * values
    return jnp.clip(values, min=-bound, max=bound).astype(held_as)


def setup_inputs(seed: int = 0) -> dict:
    key_of = jax.random.split(jax.random.key(seed), 8)
    node_feats = gaussian(key_of[0], (NODES, FEAT), 1.0, 6.0, ((0, 64),))
    tile_vals = gaussian(key_of[1], (GROUPS, N_FEAT, SPAN, SLOTS, TILE, TILE), (SPAN * SLOTS * TILE // 2) ** -0.5, 0.125, ((0, 64), (1, 2), (3, 2)))
    tile_cols = plant(jax.random.randint(key_of[2], (GROUPS, N_FEAT, SPAN, SLOTS), 0, GRP_DEV * N_FEAT), jax.random.fold_in(key_of[2], 1), 0, (GRP_DEV * N_FEAT) - 1).astype(jnp.int32)
    tile_count = plant(jax.random.randint(key_of[3], (GROUPS, N_FEAT, SPAN), 0, SLOTS + 1), jax.random.fold_in(key_of[3], 1), 0, SLOTS).astype(jnp.int32)
    node_count = plant(jax.random.randint(key_of[4], (N_TEAM,), SLAB // 2, SLAB + 1), jax.random.fold_in(key_of[4], 1), SLAB // 2, SLAB).astype(jnp.int32)
    weight = gaussian(key_of[5], (FEAT, HID), FEAT ** -0.5, 0.5)
    bias = gaussian(key_of[6], (HID,), 0.5, 3.0)
    return {"node_feats": node_feats, "tile_vals": tile_vals, "tile_cols": tile_cols, "tile_count": tile_count, "node_count": node_count, "weight": weight, "bias": bias}


def reference(node_feats, tile_vals, tile_cols, tile_count, node_count, weight, bias):
    position = jnp.arange(NODES, dtype=jnp.int32)
    live_row = (position % SLAB) < node_count[position // SLAB]
    visible = jnp.where(live_row[:, None], node_feats, jnp.zeros_like(node_feats))
    panels = visible.reshape(NODES // TILE, TILE, FEAT)
    offsets = jnp.arange(SPAN, dtype=jnp.int32) - REACH
    slot_ids = jnp.arange(SLOTS, dtype=jnp.int32)

    def one_group(group):
        slab_index = group // GRP_DEV
        col_slab = (slab_index + offsets) % N_TEAM
        col_panel = (col_slab[None, :, None] * (GRP_DEV * N_FEAT) + tile_cols[group]).astype(jnp.int32)
        live = slot_ids[None, None, :] < tile_count[group][:, :, None]
        picked = panels[col_panel].astype(jnp.float32)
        picked = jnp.where(live[..., None, None], picked, jnp.zeros_like(picked))
        tiles = tile_vals[group].astype(jnp.float32)
        return jnp.einsum("fosij,fosjc->fic", tiles, picked)

    agg = lax.map(one_group, jnp.arange(GROUPS, dtype=jnp.int32))
    agg = agg.astype(jnp.bfloat16).reshape(NODES, FEAT)
    result = jnp.dot(agg, weight, preferred_element_type=jnp.float32) + bias.astype(jnp.float32)
    result = jnp.maximum(result, 0.0)
    result = jnp.where(live_row[:, None], result, jnp.zeros_like(result))
    return result.astype(jnp.bfloat16)
```

```python
import functools

import jax
import jax.numpy as jnp
from jax import lax
from jax.experimental import pallas as pl
from jax.experimental.pallas import tpu as pltpu
from jax.sharding import PartitionSpec as P

AXES = ("team", "rep", "feat")
VMEM_LIMIT = 24 * 1024 * 1024


def permutation(move):
    teams, reps, feats = (lax.axis_size(a) for a in AXES)
    pairs = []
    for t in range(teams):
        for r in range(reps):
            for f in range(feats):
                to_t, to_r, to_f = move(t, r, f)
                pairs.append(
                    (
                        (t * reps + r) * feats + f,
                        ((to_t % teams) * reps + to_r) * feats + to_f,
                    )
                )
    return pairs


def along_ring(value):
    return lax.ppermute(value, AXES, permutation(lambda t, r, f: (t + 1 - 2 * r, r, f)))


def between_cores(value):
    return lax.ppermute(value, AXES, permutation(lambda t, r, f: (t, 1 - r, f)))


def between_feats(value):
    return lax.ppermute(value, AXES, permutation(lambda t, r, f: (t, r, 1 - f)))


def after(value, first):
    return lax.optimization_barrier((value, first))


def in_vmem(value):
    return pltpu.with_memory_space_constraint(value, pltpu.VMEM)


def in_hbm(value):
    return pltpu.with_memory_space_constraint(value, pltpu.HBM)


ON_CHIP = pl.BlockSpec(memory_space=pltpu.VMEM)
SCALARS = pl.BlockSpec(memory_space=pltpu.SMEM)
OFF_CHIP = pl.BlockSpec(memory_space=pltpu.HBM)
COST = pl.CostEstimate(flops=0, bytes_accessed=0, transcendentals=0)
PARTS = 1
OWN, NEAR, NEAR_OTHER, FAR, FAR_OTHER, KEPT, GIVEN, COLUMNS = range(8)
PARAMS = pltpu.CompilerParams(vmem_limit_bytes=VMEM_LIMIT)


def part_kernel(first, count, feats, out, held, sem):
    rows = out.shape[0]
    copy = pltpu.make_async_copy(feats.at[pl.ds(first, rows)], held, sem)
    copy.start()
    copy.wait()
    row = lax.broadcasted_iota(jnp.int32, held.shape, 0) + first
    out[...] = jnp.where(row < count[0], held[...], jnp.zeros_like(held))


def part_of_slab(node_feats, node_count, first, rows):
    shape = (rows, node_feats.shape[1])
    return pl.pallas_call(
        functools.partial(part_kernel, first),
        out_shape=pltpu.VMEM(shape, node_feats.dtype),
        in_specs=[SCALARS, OFF_CHIP],
        out_specs=ON_CHIP,
        scratch_shapes=[
            pltpu.VMEM(shape, node_feats.dtype),
            pltpu.SemaphoreType.DMA,
        ],
        compiler_params=PARAMS,
        cost_estimate=COST,
        name="part_of_slab",
    )(node_count, in_hbm(node_feats))


def place_slab(slab, panels, size):
    at = 0
    for piece in slab:
        rows = piece.shape[0]
        panels[at : at + rows, :] = piece[...]
        at += rows
    panels[at:, :] = jnp.zeros((size, panels.shape[1]), panels.dtype)


def fetch(info, steps, tiles, targets, sems):
    copies = []
    for j, step in enumerate(steps):
        source, target = tiles.at[:, 0, info[step]], targets.at[j]
        count = target.shape[0] // PARTS
        for i in range(PARTS):
            run = pl.ds(i * count, count)
            copies.append(
                pltpu.make_async_copy(source.at[run], target.at[run], sems.at[j, i])
            )
    for copy in copies:
        copy.start()
    return copies


def product_kernel(step, index, fetched, ahead, halves, info, head, tail, *refs):
    refs, panels = refs[:-1], refs[-1]
    held, tiles, total = None, None, None
    if not fetched:
        held, held_sems, refs = refs[-2], refs[-1], refs[:-2]
    if ahead:
        ahead_sems, refs = refs[-1], refs[:-1]
        later, refs = refs[-1], refs[:-1]
    outs, refs = (refs[-2:], refs[:-2]) if halves else (refs[-1:], refs[:-1])
    if fetched:
        held, refs = refs[0], refs[1:]
    if ahead or not fetched:
        tiles, refs = refs[0], refs[1:]
    if refs:
        (total,) = refs
    _, groups, slots, size, _ = held.shape
    copies = [] if fetched else fetch(info, [step], tiles, held, held_sems)
    ahead_copies = fetch(info, ahead, tiles, later, ahead_sems) if ahead else []
    place_slab((head, tail), panels, size)
    for copy in copies:
        copy.wait()
    table = COLUMNS + info[step] * (groups * slots)
    for out, start_at in zip(outs, (GIVEN, KEPT)):
        start = info[start_at] if halves else 0
        for i in range(out.shape[0]):
            g = start + i
            lhs, rhs = [], []
            for k in range(slots):
                panel = info[table + g * slots + k]
                rows = pl.ds(pl.multiple_of(panel * size, size), size)
                lhs.append(held[index, g, k])
                rhs.append(panels[rows, :])
            value = jnp.dot(
                jnp.concatenate(lhs, axis=1),
                jnp.concatenate(rhs, axis=0),
                preferred_element_type=jnp.float32,
            )
            if total is not None:
                value = value + total[g]
            out[i] = value.astype(out.dtype)
    for copy in ahead_copies:
        copy.wait()


def product(step, info, slab, tiles, total, fetched=None, index=0, ahead=(), halves=False):
    groups, _, _, slots, size, _ = tiles.shape
    rows, width = sum(piece.shape[0] for piece in slab), slab[0].shape[1]
    operands, specs = [info, *map(in_vmem, slab)], [SCALARS, ON_CHIP, ON_CHIP]
    if halves:
        out_shape = [
            pltpu.VMEM((groups // 2, size, width), dtype)
            for dtype in (jnp.bfloat16, jnp.float32)
        ]
    else:
        out_shape = [pltpu.VMEM((groups, size, width), jnp.float32)]
    scratch = []
    if fetched is not None:
        operands.append(in_vmem(fetched))
        specs.append(ON_CHIP)
    if ahead or fetched is None:
        operands.append(in_hbm(tiles))
        specs.append(OFF_CHIP)
    if total is not None:
        operands.append(in_vmem(total))
        specs.append(ON_CHIP)
    if ahead:
        shape = (len(ahead), groups, slots, size, size)
        out_shape.append(pltpu.VMEM(shape, tiles.dtype))
        scratch.append(pltpu.SemaphoreType.DMA((len(ahead), PARTS)))
    if fetched is None:
        scratch.append(pltpu.VMEM((1, groups, slots, size, size), tiles.dtype))
        scratch.append(pltpu.SemaphoreType.DMA((1, PARTS)))
    scratch.append(pltpu.VMEM((rows + size, width), slab[0].dtype))
    outs = pl.pallas_call(
        functools.partial(
            product_kernel, step, index, fetched is not None, tuple(ahead), halves
        ),
        out_shape=out_shape,
        in_specs=specs,
        out_specs=[ON_CHIP] * len(out_shape),
        scratch_shapes=scratch,
        compiler_params=PARAMS,
        cost_estimate=COST,
        name="product",
    )(*operands)
    return outs if len(outs) > 1 else outs[0]


def add_kernel(kept, got, out):
    out[...] = (kept[...] + got[...].astype(jnp.float32)).astype(out.dtype)


def add(kept, got):
    return pl.pallas_call(
        add_kernel,
        out_shape=pltpu.VMEM(got.shape, got.dtype),
        in_specs=[ON_CHIP, ON_CHIP],
        out_specs=ON_CHIP,
        compiler_params=PARAMS,
        name="add_halves",
    )(in_vmem(kept), in_vmem(got))


def finish_kernel(place, count, agg, weight, bias, *refs):
    out, held, sems = refs[-3:]
    groups, size, _ = agg.shape
    rep, feat = place[0], place[1]
    live = count[0] - rep * (2 * groups * size)
    biased = bias[...].astype(jnp.float32)
    row = lax.broadcasted_iota(jnp.int32, held.shape[1:], 0)
    copies = []
    for g in range(groups):
        start = (2 * g + feat) * size
        value = jnp.dot(agg[g], weight[...], preferred_element_type=jnp.float32)
        value = jnp.maximum(value + biased, 0.0)
        held[g] = jnp.where(row + start < live, value, 0.0).astype(out.dtype)
        target = out.at[pl.ds(pl.multiple_of(start, size), size)]
        copies.append(pltpu.make_async_copy(held.at[g], target, sems.at[g]))
        copies[-1].start()
    for copy in copies:
        copy.wait()


def finish(place, count, agg, weight, bias, out=None):
    groups, size, _ = agg.shape
    share = weight.shape[1]
    before = [] if out is None else [out]
    return pl.pallas_call(
        finish_kernel,
        out_shape=jax.ShapeDtypeStruct((groups * 2 * size, share), agg.dtype),
        in_specs=[SCALARS, SCALARS] + [ON_CHIP] * 3 + [OFF_CHIP] * len(before),
        out_specs=OFF_CHIP,
        scratch_shapes=[
            pltpu.VMEM((groups, size, share), agg.dtype),
            pltpu.SemaphoreType.DMA((groups,)),
        ],
        input_output_aliases={5: 0} if before else {},
        compiler_params=PARAMS,
        name="finish",
    )(place, count, in_vmem(agg), in_vmem(weight), in_vmem(bias), *before)


def local(node_feats, tile_vals, tile_cols, tile_count, node_count, weight, bias):
    size = tile_vals.shape[-1]
    groups, _, spans, slots = tile_vals.shape[:4]
    reach = spans // 2
    rep, feat = lax.axis_index("rep"), lax.axis_index("feat")
    panels = node_feats.shape[0] // size
    slot_ids = rep * slots + jnp.arange(slots, dtype=jnp.int32)
    live = slot_ids[None, None, :] < tile_count[:, 0, :, None]
    columns = jnp.where(live, tile_cols[:, 0], panels)
    columns = columns.transpose(1, 0, 2).reshape(-1)
    half = groups // 2
    sign = 2 * rep - 1
    steps = reach + sign * jnp.array([0, 1, -1, 2, -2], jnp.int32)
    starts = jnp.stack([rep * half, (1 - rep) * half])
    info = jnp.concatenate([steps, starts, columns]).astype(jnp.int32)
    share = weight.shape[1] // lax.axis_size("feat")
    weight_own = lax.dynamic_slice_in_dim(weight, feat * share, share, 1)
    bias_own = lax.dynamic_slice_in_dim(bias, feat * share, share, 0)[None]

    rows = node_feats.shape[0]
    cut = rows * 5 // 8 // size * size
    own = [
        part_of_slab(node_feats, node_count, 0, cut),
        part_of_slab(node_feats, node_count, cut, rows - cut),
    ]
    near = [along_ring(piece) for piece in own]
    total, tiles = product(OWN, info, own, tile_vals, None, ahead=(NEAR, NEAR_OTHER))
    first, (total, tiles) = after(near[0], (total, tiles))
    near = [first, near[1]]
    far = [along_ring(piece) for piece in near]
    near_other = [between_cores(piece) for piece in near]
    total, far_tiles = product(
        NEAR, info, near, tile_vals, total, tiles, 0, ahead=(FAR, FAR_OTHER)
    )
    total = product(NEAR_OTHER, info, near_other, tile_vals, total, tiles, 1)
    far, (total, far_tiles) = after(far, (total, far_tiles))
    far_other = [between_cores(piece) for piece in far]
    total = product(FAR, info, far, tile_vals, total, far_tiles, 0)
    given, kept = product(
        FAR_OTHER, info, far_other, tile_vals, total, far_tiles, 1, halves=True
    )
    got = between_cores(given)
    mine = add(kept, got)
    theirs = between_feats(mine)
    here = jnp.stack([rep, feat]).astype(jnp.int32)
    there = jnp.stack([rep, 1 - feat]).astype(jnp.int32)
    out = finish(here, node_count, mine, weight_own, bias_own)
    return finish(there, node_count, theirs, weight_own, bias_own, out)


def solution(mesh):
    return jax.shard_map(
        local,
        mesh=mesh,
        in_specs=(
            P("team", None),
            P("team", "feat", None, "rep", None, None),
            P("team", "feat", None, "rep"),
            P("team", "feat", None),
            P("team"),
            P(),
            P(),
        ),
        out_specs=P(("team", "rep"), "feat"),
        check_vma=False,
    )
```

```python
import functools

import jax
import jax.numpy as jnp
from jax import lax
from jax.experimental import pallas as pl
from jax.experimental.pallas import tpu as pltpu
from jax.sharding import PartitionSpec as P

AXES = ("team", "rep", "feat")
VMEM_LIMIT = 24 * 1024 * 1024


def permutation(move):
    teams, reps, feats = (lax.axis_size(a) for a in AXES)
    pairs = []
    for t in range(teams):
        for r in range(reps):
            for f in range(feats):
                to_t, to_r, to_f = move(t, r, f)
                pairs.append(
                    (
                        (t * reps + r) * feats + f,
                        ((to_t % teams) * reps + to_r) * feats + to_f,
                    )
                )
    return pairs


def along_ring(value):
    return lax.ppermute(value, AXES, permutation(lambda t, r, f: (t + 1 - 2 * r, r, f)))


def between_cores(value):
    return lax.ppermute(value, AXES, permutation(lambda t, r, f: (t, 1 - r, f)))


def between_feats(value):
    return lax.ppermute(value, AXES, permutation(lambda t, r, f: (t, r, 1 - f)))


def after(value, first):
    return lax.optimization_barrier((value, first))


def in_vmem(value):
    return pltpu.with_memory_space_constraint(value, pltpu.VMEM)


def in_hbm(value):
    return pltpu.with_memory_space_constraint(value, pltpu.HBM)


ON_CHIP = pl.BlockSpec(memory_space=pltpu.VMEM)
SCALARS = pl.BlockSpec(memory_space=pltpu.SMEM)
OFF_CHIP = pl.BlockSpec(memory_space=pltpu.HBM)
COST = pl.CostEstimate(flops=0, bytes_accessed=0, transcendentals=0)
OWN, NEAR, NEAR_OTHER, FAR, FAR_OTHER = range(5)
PARAMS = pltpu.CompilerParams(vmem_limit_bytes=VMEM_LIMIT)


def head_kernel(feats, out, sem):
    copy = pltpu.make_async_copy(feats.at[pl.ds(0, out.shape[0])], out, sem)
    copy.start()
    copy.wait()


def tail_kernel(first, count, feats, out, held, sem):
    rows = out.shape[0]
    copy = pltpu.make_async_copy(feats.at[pl.ds(first, rows)], held, sem)
    copy.start()
    copy.wait()
    row = lax.broadcasted_iota(jnp.int32, held.shape, 0) + first
    out[...] = jnp.where(row < count[0:1, :], held[...], jnp.zeros_like(held))


def split(node_feats, count):
    rows, width = node_feats.shape
    half = (rows // 2, width)
    out = pltpu.VMEM(half, node_feats.dtype)
    options = dict(
        out_shape=out,
        out_specs=ON_CHIP,
        compiler_params=PARAMS,
        cost_estimate=COST,
    )
    node_feats = in_hbm(node_feats)
    head = pl.pallas_call(
        head_kernel,
        in_specs=[OFF_CHIP],
        scratch_shapes=[pltpu.SemaphoreType.DMA],
        name="head_of_slab",
        **options,
    )(node_feats)
    tail = pl.pallas_call(
        functools.partial(tail_kernel, rows // 2),
        in_specs=[ON_CHIP, OFF_CHIP],
        scratch_shapes=[out, pltpu.SemaphoreType.DMA],
        name="tail_of_slab",
        **options,
    )(in_vmem(count), node_feats)
    return [head, tail]


def thirds_kernel(head, tail, *outs):
    at, cut = 0, head.shape[0]
    for out in outs:
        end = at + out.shape[0]
        middle = min(max(cut, at), end)
        if middle > at:
            out[: middle - at] = head[at:middle]
        if end > middle:
            out[middle - at :] = tail[middle - cut : end - cut]
        at = end


def thirds(slab, size):
    rows, width = sum(piece.shape[0] for piece in slab), slab[0].shape[1]
    less = rows // 3 // size * size
    outs = [
        pltpu.VMEM((count, width), slab[0].dtype)
        for count in (rows - 2 * less, less, less)
    ]
    return pl.pallas_call(
        thirds_kernel,
        out_shape=outs,
        in_specs=[ON_CHIP] * 2,
        out_specs=[ON_CHIP] * 3,
        compiler_params=PARAMS,
        cost_estimate=COST,
        name="thirds",
    )(*map(in_vmem, slab))


def place_slab(slab, panels, size):
    at = 0
    for piece in slab:
        rows = piece.shape[0]
        panels[at : at + rows, :] = piece[...]
        at += rows
    panels[at:, :] = jnp.zeros((size, panels.shape[1]), panels.dtype)


def offset_of(step, spans):
    sign = 2 * lax.axis_index("rep") - 1
    return spans // 2 + sign * (0, 1, -1, 2, -2)[step]


def fetch(steps, tiles, targets, sems):
    copies = []
    for j, (step, target) in enumerate(zip(steps, targets)):
        source = tiles.at[:, 0, offset_of(step, tiles.shape[2])]
        copies.append(pltpu.make_async_copy(source, target, sems.at[j]))
    for copy in copies:
        copy.start()
    return copies


def product_kernel(step, fetched, ahead, halves, pieces, spans, columns, *refs):
    refs = list(refs)
    slab = [refs.pop(0) for _ in range(pieces)]
    held = refs.pop(0) if fetched else None
    total = refs.pop(0) if fetched else None
    tiles = refs.pop(0) if ahead or not fetched else None
    outs = [refs.pop(0) for _ in range(2 if halves else 1)]
    later = [refs.pop(0) for _ in ahead]
    panels = refs.pop(0)
    copies = []
    if not fetched:
        held, held_sems = refs.pop(0), refs.pop(0)
        copies = fetch([step], tiles, [held], held_sems)
    ahead_copies = fetch(ahead, tiles, later, refs.pop(0)) if ahead else []
    groups, slots, size, _ = held.shape
    place_slab(slab, panels, size)
    for copy in copies:
        copy.wait()
    table = offset_of(step, spans) * (groups * slots)
    rep = lax.axis_index("rep")
    for out, part in zip(outs, (1 - rep, rep)):
        start = part * (groups // 2) if halves else 0
        for i in range(out.shape[0]):
            g = start + i
            lhs, rhs = [], []
            for k in range(slots):
                panel = columns[table + g * slots + k]
                rows = pl.ds(pl.multiple_of(panel * size, size), size)
                lhs.append(held[g, k])
                rhs.append(panels[rows, :])
            value = jnp.dot(
                jnp.concatenate(lhs, axis=1),
                jnp.concatenate(rhs, axis=0),
                preferred_element_type=jnp.float32,
            )
            if fetched:
                value = value + total[g]
            out[i] = value.astype(out.dtype)
    for copy in ahead_copies:
        copy.wait()


def product(step, columns, slab, tiles, held=None, total=None, ahead=(), halves=False):
    groups, _, spans, slots, size, _ = tiles.shape
    rows, width = sum(piece.shape[0] for piece in slab), slab[0].shape[1]
    fetched = held is not None
    shape = (groups, slots, size, size)
    operands = [columns, *map(in_vmem, slab)]
    specs = [SCALARS] + [ON_CHIP] * len(slab)
    if halves:
        out_shape = [
            pltpu.VMEM((groups // 2, size, width), dtype)
            for dtype in (jnp.bfloat16, jnp.float32)
        ]
    else:
        out_shape = [pltpu.VMEM((groups, size, width), jnp.float32)]
    scratch = [pltpu.VMEM((rows + size, width), slab[0].dtype)]
    if fetched:
        operands += [in_vmem(held), in_vmem(total)]
        specs += [ON_CHIP] * 2
    else:
        scratch += [pltpu.VMEM(shape, tiles.dtype), pltpu.SemaphoreType.DMA((1,))]
    if ahead or not fetched:
        operands.append(in_hbm(tiles))
        specs.append(OFF_CHIP)
    if ahead:
        out_shape += [pltpu.VMEM(shape, tiles.dtype)] * len(ahead)
        scratch.append(pltpu.SemaphoreType.DMA((len(ahead),)))
    outs = pl.pallas_call(
        functools.partial(
            product_kernel, step, fetched, tuple(ahead), halves, len(slab), spans
        ),
        out_shape=out_shape,
        in_specs=specs,
        out_specs=[ON_CHIP] * len(out_shape),
        scratch_shapes=scratch,
        compiler_params=PARAMS,
        cost_estimate=COST,
        name="product",
    )(*operands)
    return outs if len(outs) > 1 else outs[0]


def add_kernel(kept, got, out):
    out[...] = (kept[...] + got[...].astype(jnp.float32)).astype(out.dtype)


def add(kept, got):
    return pl.pallas_call(
        add_kernel,
        out_shape=pltpu.VMEM(got.shape, got.dtype),
        in_specs=[ON_CHIP, ON_CHIP],
        out_specs=ON_CHIP,
        compiler_params=PARAMS,
        name="add_halves",
    )(in_vmem(kept), in_vmem(got))


def finish_kernel(other, count, agg, weight, bias, *refs):
    out, held, sem = refs[-3:]
    groups, size, _ = agg.shape
    feat = lax.axis_index("feat")
    feat = 1 - feat if other else feat
    live = count[0:1, :] - (lax.axis_index("rep") * (2 * groups) + feat) * size
    biased = bias[...].astype(jnp.float32)
    row = lax.broadcasted_iota(jnp.int32, held.shape[1:], 0)
    for g in range(groups):
        value = jnp.dot(agg[g], weight[...], preferred_element_type=jnp.float32)
        value = jnp.maximum(value + biased, 0.0)
        held[g] = jnp.where(row + 2 * g * size < live, value, 0.0).astype(out.dtype)
    copy = pltpu.make_async_copy(held, out.at[:, feat], sem)
    copy.start()
    copy.wait()


def finish(count, agg, weight, bias, out=None):
    groups, size, _ = agg.shape
    share = weight.shape[1]
    before = [] if out is None else [out]
    return pl.pallas_call(
        functools.partial(finish_kernel, out is not None),
        out_shape=jax.ShapeDtypeStruct((groups, 2, size, share), agg.dtype),
        in_specs=[ON_CHIP] * 4 + [OFF_CHIP] * len(before),
        out_specs=OFF_CHIP,
        scratch_shapes=[
            pltpu.VMEM((groups, size, share), agg.dtype),
            pltpu.SemaphoreType.DMA,
        ],
        input_output_aliases={4: 0} if before else {},
        compiler_params=PARAMS,
        name="finish",
    )(in_vmem(count), in_vmem(agg), in_vmem(weight), in_vmem(bias), *before)


def local(node_feats, tile_vals, tile_cols, tile_count, node_count, weight, bias):
    size = tile_vals.shape[-1]
    groups, _, spans, slots = tile_vals.shape[:4]
    reach = spans // 2
    rep, feat = lax.axis_index("rep"), lax.axis_index("feat")
    panels = node_feats.shape[0] // size
    slot_ids = rep * slots + jnp.arange(slots, dtype=jnp.int32)
    live = slot_ids[None, None, :] < tile_count[:, 0, :, None]
    columns = jnp.where(live, tile_cols[:, 0], panels)
    columns = columns.transpose(1, 0, 2).reshape(-1).astype(jnp.int32)
    share = weight.shape[1] // lax.axis_size("feat")
    weight_own = lax.dynamic_slice_in_dim(weight, feat * share, share, 1)
    bias_own = lax.dynamic_slice_in_dim(bias, feat * share, share, 0)[None]

    count = jnp.broadcast_to(node_count[None], (8, node_feats.shape[1]))
    own = split(node_feats, count)
    near = [along_ring(piece) for piece in own]
    total, near_tiles, near_other_tiles = product(
        OWN, columns, own, tile_vals, ahead=(NEAR, NEAR_OTHER)
    )
    first, (total, near_tiles, near_other_tiles) = after(
        near[0], (total, near_tiles, near_other_tiles)
    )
    near = [first, near[1]]
    far = [along_ring(piece) for piece in near]
    near_other = [between_cores(piece) for piece in thirds(near, size)]
    total, far_tiles, far_other_tiles = product(
        NEAR, columns, near, tile_vals, near_tiles, total, ahead=(FAR, FAR_OTHER)
    )
    total = product(NEAR_OTHER, columns, near_other, tile_vals, near_other_tiles, total)
    first, total = after(far[0], total)
    far = [first, far[1]]
    far_other = [between_cores(piece) for piece in far]
    total = product(FAR, columns, far, tile_vals, far_tiles, total)
    given, kept = product(
        FAR_OTHER, columns, far_other, tile_vals, far_other_tiles, total, halves=True
    )
    got = between_cores(given)
    mine = add(kept, got)
    theirs = between_feats(mine)
    out = finish(count, mine, weight_own, bias_own)
    out = finish(count, theirs, weight_own, bias_own, out)
    return out.reshape(-1, share)


def solution(mesh):
    return jax.shard_map(
        local,
        mesh=mesh,
        in_specs=(
            P("team", None),
            P("team", "feat", None, "rep", None, None),
            P("team", "feat", None, "rep"),
            P("team", "feat", None),
            P("team"),
            P(),
            P(),
        ),
        out_specs=P(("team", "rep"), "feat"),
        check_vma=False,
    )
```

```python
import functools

import jax
import jax.numpy as jnp
from jax import lax
from jax.experimental import pallas as pl
from jax.experimental.pallas import tpu as pltpu
from jax.sharding import PartitionSpec as P

AXES = ("team", "rep", "feat")
VMEM_LIMIT = 24 * 1024 * 1024


def permutation(move):
    teams, reps, feats = (lax.axis_size(a) for a in AXES)
    pairs = []
    for t in range(teams):
        for r in range(reps):
            for f in range(feats):
                to_t, to_r, to_f = move(t, r, f)
                pairs.append(
                    (
                        (t * reps + r) * feats + f,
                        ((to_t % teams) * reps + to_r) * feats + to_f,
                    )
                )
    return pairs


def along_ring(value):
    return lax.ppermute(value, AXES, permutation(lambda t, r, f: (t + 1 - 2 * r, r, f)))


def further_along(value):
    return lax.ppermute(value, AXES, permutation(lambda t, r, f: (t + 1 - 2 * r, 1 - r, f)))


def between_cores(value):
    return lax.ppermute(value, AXES, permutation(lambda t, r, f: (t, 1 - r, f)))


def between_feats(value):
    return lax.ppermute(value, AXES, permutation(lambda t, r, f: (t, r, 1 - f)))


def after(value, first):
    return lax.optimization_barrier((value, first))


def in_vmem(value):
    return pltpu.with_memory_space_constraint(value, pltpu.VMEM)


def in_hbm(value):
    return pltpu.with_memory_space_constraint(value, pltpu.HBM)


ON_CHIP = pl.BlockSpec(memory_space=pltpu.VMEM)
SCALARS = pl.BlockSpec(memory_space=pltpu.SMEM)
OFF_CHIP = pl.BlockSpec(memory_space=pltpu.HBM)
COST = pl.CostEstimate(flops=0, bytes_accessed=0, transcendentals=0)
OWN, NEAR, NEAR_OTHER, FAR, FAR_OTHER = range(5)
PARAMS = pltpu.CompilerParams(vmem_limit_bytes=VMEM_LIMIT)


def head_kernel(feats, out, sem):
    copy = pltpu.make_async_copy(feats.at[pl.ds(0, out.shape[0])], out, sem)
    copy.start()
    copy.wait()


def tail_kernel(first, count, feats, out, held, sem):
    rows = out.shape[0]
    copy = pltpu.make_async_copy(feats.at[pl.ds(first, rows)], held, sem)
    copy.start()
    copy.wait()
    row = lax.broadcasted_iota(jnp.int32, held.shape, 0) + first
    out[...] = jnp.where(row < count[0:1, :], held[...], jnp.zeros_like(held))


def split(node_feats, count):
    rows, width = node_feats.shape
    half = (rows // 2, width)
    out = pltpu.VMEM(half, node_feats.dtype)
    options = dict(
        out_shape=out,
        out_specs=ON_CHIP,
        compiler_params=PARAMS,
        cost_estimate=COST,
    )
    node_feats = in_hbm(node_feats)
    head = pl.pallas_call(
        head_kernel,
        in_specs=[OFF_CHIP],
        scratch_shapes=[pltpu.SemaphoreType.DMA],
        name="head_of_slab",
        **options,
    )(node_feats)
    tail = pl.pallas_call(
        functools.partial(tail_kernel, rows // 2),
        in_specs=[ON_CHIP, OFF_CHIP],
        scratch_shapes=[out, pltpu.SemaphoreType.DMA],
        name="tail_of_slab",
        **options,
    )(in_vmem(count), node_feats)
    return [head, tail]


def thirds_kernel(head, tail, *outs):
    at, cut = 0, head.shape[0]
    for out in outs:
        end = at + out.shape[0]
        middle = min(max(cut, at), end)
        if middle > at:
            out[: middle - at] = head[at:middle]
        if end > middle:
            out[middle - at :] = tail[middle - cut : end - cut]
        at = end


def thirds(slab, size):
    rows, width = sum(piece.shape[0] for piece in slab), slab[0].shape[1]
    less = rows // 3 // size * size
    outs = [
        pltpu.VMEM((count, width), slab[0].dtype)
        for count in (rows - 2 * less, less, less)
    ]
    return pl.pallas_call(
        thirds_kernel,
        out_shape=outs,
        in_specs=[ON_CHIP] * 2,
        out_specs=[ON_CHIP] * 3,
        compiler_params=PARAMS,
        cost_estimate=COST,
        name="thirds",
    )(*map(in_vmem, slab))


def place_slab(slab, panels, size):
    at = 0
    for piece in slab:
        rows = piece.shape[0]
        panels[at : at + rows, :] = piece[...]
        at += rows
    panels[at:, :] = jnp.zeros((size, panels.shape[1]), panels.dtype)


def offset_of(step, spans):
    sign = 2 * lax.axis_index("rep") - 1
    return spans // 2 + sign * (0, 1, -1, -2, 2)[step]


def fetch(steps, tiles, targets, sems):
    copies = []
    for j, (step, target) in enumerate(zip(steps, targets)):
        source = tiles.at[:, 0, offset_of(step, tiles.shape[2])]
        copies.append(pltpu.make_async_copy(source, target, sems.at[j]))
    for copy in copies:
        copy.start()
    return copies


def product_kernel(step, fetched, ahead, last, part, pieces, spans, columns, *refs):
    refs = list(refs)
    slab = [refs.pop(0) for _ in range(pieces)]
    held = refs.pop(0) if fetched else None
    total = refs.pop(0) if fetched else None
    tiles = refs.pop(0) if ahead or not fetched else None
    split_out = last and not ahead
    outs = [refs.pop(0) for _ in range(2 if split_out else 1)]
    later = [refs.pop(0) for _ in range(len(ahead) + (last and bool(ahead)))]
    panels, table, table_sem = refs.pop(0), refs.pop(0), refs.pop(0)
    table_copy = pltpu.make_async_copy(columns, table, table_sem)
    table_copy.start()
    rep = lax.axis_index("rep")
    copies = []
    if not fetched:
        held, held_sems = refs.pop(0), refs.pop(0)
        copies = fetch([step], tiles, [held], held_sems)
    ahead_copies = []
    if ahead:
        sems = refs.pop(0)
        whole = ahead[:-1] if last else ahead
        ahead_copies = fetch(whole, tiles, later, sems)
        if last:
            source = tiles.at[:, 0, offset_of(ahead[-1], spans)]
            for i, target in enumerate(later[-2:]):
                count = target.shape[0]
                half = source.at[pl.ds((1 - rep, rep)[i] * count, count)]
                sem = sems.at[len(whole) + i]
                ahead_copies.append(pltpu.make_async_copy(half, target, sem))
                ahead_copies[-1].start()
    _, slots, size, _ = held.shape
    groups = table.shape[0] // (spans * slots)
    place_slab(slab, panels, size)
    table_copy.wait()
    for copy in copies:
        copy.wait()
    first = offset_of(step, spans) * (groups * slots)
    for j, out in enumerate(outs):
        halved = split_out or part is not None
        start = (1 - rep, rep)[part or j] * (groups // 2) if halved else 0
        for i in range(out.shape[0]):
            at = i if part is not None else start + i
            lhs, rhs = [], []
            for k in range(slots):
                panel = table[first + (start + i) * slots + k]
                rows = pl.ds(pl.multiple_of(panel * size, size), size)
                lhs.append(held[at, k])
                rhs.append(panels[rows, :])
            value = jnp.dot(
                jnp.concatenate(lhs, axis=1),
                jnp.concatenate(rhs, axis=0),
                preferred_element_type=jnp.float32,
            )
            if fetched:
                value = value + total[at]
            out[i] = value.astype(out.dtype)
    for copy in ahead_copies:
        copy.wait()


def product(
    step, columns, slab, tiles, held=None, total=None, ahead=(), last=False, part=None
):
    groups, _, spans, slots, size, _ = tiles.shape
    rows, width = sum(piece.shape[0] for piece in slab), slab[0].shape[1]
    fetched = held is not None
    shape, half = (groups, slots, size, size), (groups // 2, slots, size, size)
    operands = [columns, *map(in_vmem, slab)]
    specs = [pl.BlockSpec(memory_space=pl.ANY)] + [ON_CHIP] * len(slab)
    sums = pltpu.VMEM((groups, size, width), jnp.float32)
    half_sums = pltpu.VMEM((groups // 2, size, width), jnp.float32)
    out_shape = [sums]
    if part is not None:
        dtype = (jnp.bfloat16, jnp.float32)[part]
        out_shape = [pltpu.VMEM((groups // 2, size, width), dtype)]
    elif last and not ahead:
        out_shape = [half_sums] * 2
    scratch = [
        pltpu.VMEM((rows + size, width), slab[0].dtype),
        pltpu.SMEM(columns.shape, columns.dtype),
        pltpu.SemaphoreType.DMA,
    ]
    if fetched:
        operands += [in_vmem(held), in_vmem(total)]
        specs += [ON_CHIP] * 2
    else:
        scratch += [pltpu.VMEM(shape, tiles.dtype), pltpu.SemaphoreType.DMA((1,))]
    if ahead or not fetched:
        operands.append(in_hbm(tiles))
        specs.append(OFF_CHIP)
    if ahead:
        later = [shape] * (len(ahead) - last) + [half] * (2 * last)
        out_shape += [pltpu.VMEM(each, tiles.dtype) for each in later]
        scratch.append(pltpu.SemaphoreType.DMA((len(later),)))
    outs = pl.pallas_call(
        functools.partial(
            product_kernel, step, fetched, tuple(ahead), last, part, len(slab), spans
        ),
        out_shape=out_shape,
        in_specs=specs,
        out_specs=[ON_CHIP] * len(out_shape),
        scratch_shapes=scratch,
        compiler_params=PARAMS,
        cost_estimate=COST,
        name="product",
    )(*operands)
    return outs if len(outs) > 1 else outs[0]


def add_kernel(kept, got, out):
    out[...] = (kept[...] + got[...].astype(jnp.float32)).astype(out.dtype)


def add(kept, got):
    return pl.pallas_call(
        add_kernel,
        out_shape=pltpu.VMEM(got.shape, got.dtype),
        in_specs=[ON_CHIP, ON_CHIP],
        out_specs=ON_CHIP,
        compiler_params=PARAMS,
        name="add_halves",
    )(in_vmem(kept), in_vmem(got))


def finish_kernel(other, count, agg, weight, bias, *refs):
    out, held, sem = refs[-3:]
    groups, size, _ = agg.shape
    feat = lax.axis_index("feat")
    feat = 1 - feat if other else feat
    live = count[0:1, :] - (lax.axis_index("rep") * (2 * groups) + feat) * size
    biased = bias[...].astype(jnp.float32)
    row = lax.broadcasted_iota(jnp.int32, held.shape[1:], 0)
    for g in range(groups):
        value = jnp.dot(agg[g], weight[...], preferred_element_type=jnp.float32)
        value = jnp.maximum(value + biased, 0.0)
        held[g] = jnp.where(row + 2 * g * size < live, value, 0.0).astype(out.dtype)
    copy = pltpu.make_async_copy(held, out.at[:, feat], sem)
    copy.start()
    copy.wait()


def finish(count, agg, weight, bias, out=None):
    groups, size, _ = agg.shape
    share = weight.shape[1]
    before = [] if out is None else [out]
    return pl.pallas_call(
        functools.partial(finish_kernel, out is not None),
        out_shape=jax.ShapeDtypeStruct((groups, 2, size, share), agg.dtype),
        in_specs=[ON_CHIP] * 4 + [OFF_CHIP] * len(before),
        out_specs=OFF_CHIP,
        scratch_shapes=[
            pltpu.VMEM((groups, size, share), agg.dtype),
            pltpu.SemaphoreType.DMA,
        ],
        input_output_aliases={4: 0} if before else {},
        compiler_params=PARAMS,
        name="finish",
    )(in_vmem(count), in_vmem(agg), in_vmem(weight), in_vmem(bias), *before)


def local(node_feats, tile_vals, tile_cols, tile_count, node_count, weight, bias):
    size = tile_vals.shape[-1]
    groups, _, spans, slots = tile_vals.shape[:4]
    reach = spans // 2
    rep, feat = lax.axis_index("rep"), lax.axis_index("feat")
    panels = node_feats.shape[0] // size
    slot_ids = rep * slots + jnp.arange(slots, dtype=jnp.int32)
    live = slot_ids[None, None, :] < tile_count[:, 0, :, None]
    columns = jnp.where(live, tile_cols[:, 0], panels)
    columns = columns.transpose(1, 0, 2).reshape(-1).astype(jnp.int32)
    share = weight.shape[1] // lax.axis_size("feat")
    weight_own = lax.dynamic_slice_in_dim(weight, feat * share, share, 1)
    bias_own = lax.dynamic_slice_in_dim(bias, feat * share, share, 0)[None]

    count = jnp.broadcast_to(node_count[None], (8, node_feats.shape[1]))
    own = split(node_feats, count)
    near = [along_ring(piece) for piece in own]
    total, near_tiles, near_other_tiles = product(
        OWN, columns, own, tile_vals, ahead=(NEAR, NEAR_OTHER)
    )
    first, (total, near_tiles, near_other_tiles) = after(
        near[0], (total, near_tiles, near_other_tiles)
    )
    near = [first, near[1]]
    far = [further_along(piece) for piece in near]
    near_other = [between_cores(piece) for piece in thirds(near, size)]
    total, far_tiles, *far_other_tiles = product(
        NEAR, columns, near, tile_vals, near_tiles, total, (FAR, FAR_OTHER), last=True
    )
    total = product(NEAR_OTHER, columns, near_other, tile_vals, near_other_tiles, total)
    first, total = after(far[0], total)
    far = [first, far[1]]
    far_other = [between_cores(piece) for piece in far]
    totals = product(FAR, columns, far, tile_vals, far_tiles, total, last=True)
    given, kept = (
        product(
            FAR_OTHER, columns, far_other, tile_vals, far_other_tiles[i], totals[i], part=i
        )
        for i in range(2)
    )
    got = between_cores(given)
    mine = add(kept, got)
    theirs = between_feats(mine)
    out = finish(count, mine, weight_own, bias_own)
    out = finish(count, theirs, weight_own, bias_own, out)
    return out.reshape(-1, share)


def solution(mesh):
    return jax.shard_map(
        local,
        mesh=mesh,
        in_specs=(
            P("team", None),
            P("team", "feat", None, "rep", None, None),
            P("team", "feat", None, "rep"),
            P("team", "feat", None),
            P("team"),
            P(),
            P(),
        ),
        out_specs=P(("team", "rep"), "feat"),
        check_vma=False,
    )
```

```python
import functools

import jax
import jax.numpy as jnp
from jax import lax
from jax.experimental import pallas as pl
from jax.experimental.pallas import tpu as pltpu
from jax.sharding import PartitionSpec as P

AXES = ("team", "rep", "feat")
VMEM_LIMIT = 24 * 1024 * 1024


def permutation(move):
    teams, reps, feats = (lax.axis_size(a) for a in AXES)
    pairs = []
    for t in range(teams):
        for r in range(reps):
            for f in range(feats):
                to_t, to_r, to_f = move(t, r, f)
                pairs.append(
                    (
                        (t * reps + r) * feats + f,
                        ((to_t % teams) * reps + to_r) * feats + to_f,
                    )
                )
    return pairs


def along_ring(value):
    return lax.ppermute(value, AXES, permutation(lambda t, r, f: (t + 1 - 2 * r, r, f)))


def further_along(value):
    return lax.ppermute(value, AXES, permutation(lambda t, r, f: (t + 1 - 2 * r, 1 - r, f)))


def between_cores(value):
    return lax.ppermute(value, AXES, permutation(lambda t, r, f: (t, 1 - r, f)))


def between_feats(value):
    return lax.ppermute(value, AXES, permutation(lambda t, r, f: (t, r, 1 - f)))


def after(value, first):
    return lax.optimization_barrier((value, first))


def in_vmem(value):
    return pltpu.with_memory_space_constraint(value, pltpu.VMEM)


def in_smem(value):
    return pltpu.with_memory_space_constraint(value, pltpu.SMEM)


def in_hbm(value):
    return pltpu.with_memory_space_constraint(value, pltpu.HBM)


ON_CHIP = pl.BlockSpec(memory_space=pltpu.VMEM)
SCALARS = pl.BlockSpec(memory_space=pltpu.SMEM)
OFF_CHIP = pl.BlockSpec(memory_space=pltpu.HBM)
COST = pl.CostEstimate(flops=0, bytes_accessed=0, transcendentals=0)
OWN, NEAR, NEAR_OTHER, FAR, FAR_OTHER = range(5)
GIVEN, KEPT = range(2)
GIFTS = 2
PARAMS = pltpu.CompilerParams(vmem_limit_bytes=VMEM_LIMIT)


def head_kernel(feats, out, sem):
    copy = pltpu.make_async_copy(feats.at[pl.ds(0, out.shape[0])], out, sem)
    copy.start()
    copy.wait()


def tail_kernel(first, count, feats, out, held, sem):
    rows = out.shape[0]
    copy = pltpu.make_async_copy(feats.at[pl.ds(first, rows)], held, sem)
    copy.start()
    copy.wait()
    row = lax.broadcasted_iota(jnp.int32, held.shape, 0) + first
    out[...] = jnp.where(row < count[0:1, :], held[...], jnp.zeros_like(held))


def split(node_feats, count):
    rows, width = node_feats.shape
    half = (rows // 2, width)
    out = pltpu.VMEM(half, node_feats.dtype)
    options = dict(
        out_shape=out,
        out_specs=ON_CHIP,
        compiler_params=PARAMS,
        cost_estimate=COST,
    )
    node_feats = in_hbm(node_feats)
    head = pl.pallas_call(
        head_kernel,
        in_specs=[OFF_CHIP],
        scratch_shapes=[pltpu.SemaphoreType.DMA],
        name="head_of_slab",
        **options,
    )(node_feats)
    tail = pl.pallas_call(
        functools.partial(tail_kernel, rows // 2),
        in_specs=[ON_CHIP, OFF_CHIP],
        scratch_shapes=[out, pltpu.SemaphoreType.DMA],
        name="tail_of_slab",
        **options,
    )(in_vmem(count), node_feats)
    return [head, tail]


def thirds_kernel(head, tail, *outs):
    at, cut = 0, head.shape[0]
    for out in outs:
        end = at + out.shape[0]
        middle = min(max(cut, at), end)
        if middle > at:
            out[: middle - at] = head[at:middle]
        if end > middle:
            out[middle - at :] = tail[middle - cut : end - cut]
        at = end


def thirds(slab, size):
    rows, width = sum(piece.shape[0] for piece in slab), slab[0].shape[1]
    less = rows // 3 // size * size
    outs = [
        pltpu.VMEM((count, width), slab[0].dtype)
        for count in (rows - 2 * less, less, less)
    ]
    return pl.pallas_call(
        thirds_kernel,
        out_shape=outs,
        in_specs=[ON_CHIP] * 2,
        out_specs=[ON_CHIP] * 3,
        compiler_params=PARAMS,
        cost_estimate=COST,
        name="thirds",
    )(*map(in_vmem, slab))


def place_slab(slab, panels, size):
    at = 0
    for piece in slab:
        rows = piece.shape[0]
        panels[at : at + rows, :] = piece[...]
        at += rows
    panels[at:, :] = jnp.zeros((size, panels.shape[1]), panels.dtype)


def offset_of(step, spans):
    sign = 2 * lax.axis_index("rep") - 1
    return spans // 2 + sign * (0, 1, -1, -2, 2)[step]


def table_kernel(columns, out, sem):
    copy = pltpu.make_async_copy(columns, out, sem)
    copy.start()
    copy.wait()


def table_of(columns):
    return pl.pallas_call(
        table_kernel,
        out_shape=pltpu.SMEM(columns.shape, columns.dtype),
        in_specs=[pl.BlockSpec(memory_space=pl.ANY)],
        out_specs=SCALARS,
        scratch_shapes=[pltpu.SemaphoreType.DMA],
        compiler_params=PARAMS,
        cost_estimate=COST,
        name="table",
    )(columns)


def terms(panels, table, first, slots, tiles, at):
    size = tiles.shape[-1]
    rhs = []
    for k in range(slots):
        rows = pl.ds(pl.multiple_of(table[first + k] * size, size), size)
        rhs.append(panels[rows, :])
    return [tiles[at, k] for k in range(slots)], rhs


def multiplied(lhs, rhs):
    return jnp.dot(
        jnp.concatenate(lhs, axis=1),
        jnp.concatenate(rhs, axis=0),
        preferred_element_type=jnp.float32,
    )


def halves(groups):
    rep = lax.axis_index("rep")
    return (1 - rep) * (groups // 2), rep * (groups // 2)


def product_kernel(step, fetched, ahead, parts, halved, pieces, spans, table, *refs):
    refs = list(refs)
    slab = [refs.pop(0) for _ in range(pieces)]
    held = refs.pop(0) if fetched else None
    total = refs.pop(0) if fetched else None
    tiles = refs.pop(0) if ahead or parts or not fetched else None
    outs = [refs.pop(0) for _ in range(2 if halved else 1)]
    later = [refs.pop(0) for _ in ahead]
    part_refs = [[refs.pop(0) for _ in range(runs)] for _, _, runs in parts]
    panels, sems = refs.pop(0), refs.pop(0)
    if not fetched:
        held = refs.pop(0)
    groups, slots, size, _ = held.shape
    copies = []
    if not fetched:
        copies.append((tiles.at[:, 0, offset_of(step, spans)], held))
    now = len(copies)
    for other, target in zip(ahead, later):
        copies.append((tiles.at[:, 0, offset_of(other, spans)], target))
    for (other, half, _), targets in zip(parts, part_refs):
        for i, target in enumerate(targets):
            count = target.shape[0]
            run = pl.ds(halves(groups)[half] + i * count, count)
            copies.append((tiles.at[run, 0, offset_of(other, spans)], target))
    copies = [
        pltpu.make_async_copy(source, target, sems.at[i])
        for i, (source, target) in enumerate(copies)
    ]
    for copy in copies:
        copy.start()
    place_slab(slab, panels, size)
    for copy in copies[:now]:
        copy.wait()
    first = offset_of(step, spans) * (groups * slots)
    for out, start in zip(outs, halves(groups) if halved else (0,)):
        for i in range(out.shape[0]):
            g = start + i
            value = multiplied(*terms(panels, table, first + g * slots, slots, held, g))
            if fetched:
                value = value + total[g]
            out[i] = value.astype(out.dtype)
    for copy in copies[now:]:
        copy.wait()


def product(
    step, table, slab, tiles, held=None, total=None, ahead=(), parts=(), halved=False
):
    groups, _, spans, slots, size, _ = tiles.shape
    rows, width = sum(piece.shape[0] for piece in slab), slab[0].shape[1]
    fetched = held is not None
    shape = (groups, slots, size, size)
    operands = [in_smem(table), *map(in_vmem, slab)]
    specs = [SCALARS] + [ON_CHIP] * len(slab)
    if fetched:
        operands += [in_vmem(held), in_vmem(total)]
        specs += [ON_CHIP] * 2
    if ahead or parts or not fetched:
        operands.append(in_hbm(tiles))
        specs.append(OFF_CHIP)
    panels = pltpu.VMEM((rows + size, width), slab[0].dtype)
    count = groups // 2 if halved else groups
    out_shape = [pltpu.VMEM((count, size, width), jnp.float32)] * (groups // count)
    out_shape += [pltpu.VMEM(shape, tiles.dtype)] * len(ahead)
    for _, _, runs in parts:
        run = (groups // 2 // runs, *shape[1:])
        out_shape += [pltpu.VMEM(run, tiles.dtype)] * runs
    later = len(ahead) + sum(runs for _, _, runs in parts)
    scratch = [panels, pltpu.SemaphoreType.DMA((1 + later,))]
    if not fetched:
        scratch.append(pltpu.VMEM(shape, tiles.dtype))
    outs = pl.pallas_call(
        functools.partial(
            product_kernel, step, fetched, ahead, parts, halved, len(slab), spans
        ),
        out_shape=out_shape,
        in_specs=specs,
        out_specs=[ON_CHIP] * len(out_shape),
        scratch_shapes=scratch,
        compiler_params=PARAMS,
        cost_estimate=COST,
        name="product",
    )(*operands)
    return outs if len(outs) > 1 else outs[0]


def half_kernel(half, pieces, works, spans, *refs):
    refs = list(refs)
    tables = [refs.pop(0) for _ in works]
    slab = [refs.pop(0) for _ in range(pieces or 1)]
    tiles = [[refs.pop(0) for _ in range(count)] for _, count in works]
    total, out = refs.pop(0), refs.pop(0)
    groups, size, _ = out.shape
    panels = slab[0]
    if pieces:
        panels = refs.pop(0)
        place_slab(slab, panels, size)
    start = halves(2 * groups)[half]
    for g in range(groups):
        lhs, rhs = [], []
        for table, (step, count), runs in zip(tables, works, tiles):
            slots, run = runs[0].shape[1], groups // count
            first = (offset_of(step, spans) * (2 * groups) + start + g) * slots
            more = terms(panels, table, first, slots, runs[g // run], g % run)
            lhs, rhs = lhs + more[0], rhs + more[1]
        out[g] = (total[g] + multiplied(lhs, rhs)).astype(out.dtype)


def half_product(half, slab, works, total, spans, dtype=jnp.float32, placed=None):
    _, size, width = total.shape
    rows = sum(piece.shape[0] for piece in slab) + (0 if placed else size)
    tables = [in_smem(table) for _, table, _ in works]
    vmem = [*slab, *(runs for _, _, tiles in works for runs in tiles), total]
    out_shape = [pltpu.VMEM(total.shape, dtype)]
    panels, scratch = pltpu.VMEM((rows, width), slab[0].dtype), []
    if placed is None:
        scratch.append(panels)
    elif not placed:
        out_shape.append(panels)
    outs = pl.pallas_call(
        functools.partial(
            half_kernel,
            half,
            0 if placed else len(slab),
            [(step, len(tiles)) for step, _, tiles in works],
            spans,
        ),
        out_shape=out_shape,
        in_specs=[SCALARS] * len(tables) + [ON_CHIP] * len(vmem),
        out_specs=[ON_CHIP] * len(out_shape),
        scratch_shapes=scratch,
        compiler_params=PARAMS,
        cost_estimate=COST,
        name="half_product",
    )(*tables, *map(in_vmem, vmem))
    return outs if len(outs) > 1 else outs[0]


def add_kernel(kept, got, out):
    out[...] = (kept[...] + got[...].astype(jnp.float32)).astype(out.dtype)


def add(kept, got):
    return pl.pallas_call(
        add_kernel,
        out_shape=pltpu.VMEM(got.shape, got.dtype),
        in_specs=[ON_CHIP, ON_CHIP],
        out_specs=ON_CHIP,
        compiler_params=PARAMS,
        name="add_halves",
    )(in_vmem(kept), in_vmem(got))


def finish_kernel(other, count, agg, weight, bias, *refs):
    out, held, sem = refs[-3:]
    groups, size, _ = agg.shape
    feat = lax.axis_index("feat")
    feat = 1 - feat if other else feat
    live = count[0:1, :] - (lax.axis_index("rep") * (2 * groups) + feat) * size
    biased = bias[...].astype(jnp.float32)
    row = lax.broadcasted_iota(jnp.int32, held.shape[1:], 0)
    for g in range(groups):
        value = jnp.dot(agg[g], weight[...], preferred_element_type=jnp.float32)
        value = jnp.maximum(value + biased, 0.0)
        held[g] = jnp.where(row + 2 * g * size < live, value, 0.0).astype(out.dtype)
    copy = pltpu.make_async_copy(held, out.at[:, feat], sem)
    copy.start()
    copy.wait()


def finish(count, agg, weight, bias, out=None):
    groups, size, _ = agg.shape
    share = weight.shape[1]
    before = [] if out is None else [out]
    return pl.pallas_call(
        functools.partial(finish_kernel, out is not None),
        out_shape=jax.ShapeDtypeStruct((groups, 2, size, share), agg.dtype),
        in_specs=[ON_CHIP] * 4 + [OFF_CHIP] * len(before),
        out_specs=OFF_CHIP,
        scratch_shapes=[
            pltpu.VMEM((groups, size, share), agg.dtype),
            pltpu.SemaphoreType.DMA,
        ],
        input_output_aliases={4: 0} if before else {},
        compiler_params=PARAMS,
        name="finish",
    )(in_vmem(count), in_vmem(agg), in_vmem(weight), in_vmem(bias), *before)


def local(node_feats, tile_vals, tile_cols, tile_count, node_count, weight, bias):
    size = tile_vals.shape[-1]
    groups, _, spans, slots = tile_vals.shape[:4]
    reach = spans // 2
    rep, feat = lax.axis_index("rep"), lax.axis_index("feat")
    panels = node_feats.shape[0] // size
    slot_ids = rep * slots + jnp.arange(slots, dtype=jnp.int32)
    live = slot_ids[None, None, :] < tile_count[:, 0, :, None]
    columns = jnp.where(live, tile_cols[:, 0], panels)
    columns = columns.transpose(1, 0, 2).reshape(-1).astype(jnp.int32)
    share = weight.shape[1] // lax.axis_size("feat")
    weight_own = lax.dynamic_slice_in_dim(weight, feat * share, share, 1)
    bias_own = lax.dynamic_slice_in_dim(bias, feat * share, share, 0)[None]

    count = jnp.broadcast_to(node_count[None], (8, node_feats.shape[1]))
    own = split(node_feats, count)
    near = [along_ring(piece) for piece in own]
    table = table_of(columns)
    total, near_tiles, near_other_tiles, *gifts = product(
        OWN,
        table,
        own,
        tile_vals,
        ahead=(NEAR, NEAR_OTHER),
        parts=((FAR_OTHER, GIVEN, GIFTS),),
    )
    gifts = [between_cores(gift) for gift in gifts]
    other_columns = between_cores(columns)
    first, (total, near_tiles, near_other_tiles) = after(
        near[0], (total, near_tiles, near_other_tiles)
    )
    near = [first, near[1]]
    far = [further_along(piece) for piece in near]
    near_other = [between_cores(piece) for piece in thirds(near, size)]
    near_tiles, (gifts, other_columns) = after(near_tiles, (gifts, other_columns))
    total, far_given_tiles, far_kept_tiles, far_other_tiles = product(
        NEAR,
        table,
        near,
        tile_vals,
        near_tiles,
        total,
        parts=((FAR, GIVEN, 1), (FAR, KEPT, 1), (FAR_OTHER, KEPT, 1)),
    )
    total, other_table = after(total, table_of(other_columns))
    totals = product(
        NEAR_OTHER, table, near_other, tile_vals, near_other_tiles, total, halved=True
    )
    first, totals = after(far[0], totals)
    far = [first, far[1]]
    far_other = [between_cores(piece) for piece in far]
    given, far_panels = half_product(
        GIVEN,
        far,
        [(FAR, table, [far_given_tiles])],
        totals[0],
        spans,
        jnp.bfloat16,
        placed=False,
    )
    got = between_cores(given)
    works = [(FAR, table, [far_kept_tiles]), (FAR, other_table, gifts)]
    kept = half_product(KEPT, [far_panels], works, totals[1], spans, placed=True)
    works = [(FAR_OTHER, table, [far_other_tiles])]
    kept = half_product(KEPT, far_other, works, kept, spans)
    mine = add(kept, got)
    theirs = between_feats(mine)
    out = finish(count, mine, weight_own, bias_own)
    out = finish(count, theirs, weight_own, bias_own, out)
    return out.reshape(-1, share)


def solution(mesh):
    return jax.shard_map(
        local,
        mesh=mesh,
        in_specs=(
            P("team", None),
            P("team", "feat", None, "rep", None, None),
            P("team", "feat", None, "rep"),
            P("team", "feat", None),
            P("team"),
            P(),
            P(),
        ),
        out_specs=P(("team", "rep"), "feat"),
        check_vma=False,
    )
```

```python
import functools

import jax
import jax.numpy as jnp
from jax import lax
from jax.experimental import pallas as pl
from jax.experimental.pallas import tpu as pltpu
from jax.sharding import PartitionSpec as P

AXES = ("team", "rep", "feat")
VMEM_LIMIT = 24 * 1024 * 1024


def permutation(move):
    teams, reps, feats = (lax.axis_size(a) for a in AXES)
    pairs = []
    for t in range(teams):
        for r in range(reps):
            for f in range(feats):
                to_t, to_r, to_f = move(t, r, f)
                pairs.append(
                    (
                        (t * reps + r) * feats + f,
                        ((to_t % teams) * reps + to_r) * feats + to_f,
                    )
                )
    return pairs


def along_ring(value):
    return lax.ppermute(value, AXES, permutation(lambda t, r, f: (t + 1 - 2 * r, r, f)))


def further_along(value):
    return lax.ppermute(value, AXES, permutation(lambda t, r, f: (t + 1 - 2 * r, 1 - r, f)))


def between_cores(value):
    return lax.ppermute(value, AXES, permutation(lambda t, r, f: (t, 1 - r, f)))


def between_feats(value):
    return lax.ppermute(value, AXES, permutation(lambda t, r, f: (t, r, 1 - f)))


def after(value, first):
    return lax.optimization_barrier((value, first))


def in_vmem(value):
    return pltpu.with_memory_space_constraint(value, pltpu.VMEM)


def in_smem(value):
    return pltpu.with_memory_space_constraint(value, pltpu.SMEM)


def in_hbm(value):
    return pltpu.with_memory_space_constraint(value, pltpu.HBM)


ON_CHIP = pl.BlockSpec(memory_space=pltpu.VMEM)
SCALARS = pl.BlockSpec(memory_space=pltpu.SMEM)
OFF_CHIP = pl.BlockSpec(memory_space=pltpu.HBM)
COST = pl.CostEstimate(flops=0, bytes_accessed=0, transcendentals=0)
OWN, NEAR, NEAR_OTHER, FAR, FAR_OTHER = range(5)
GIVEN, KEPT = range(2)
GIFTS = 2
PARAMS = pltpu.CompilerParams(vmem_limit_bytes=VMEM_LIMIT)


def head_kernel(feats, out, sems):
    runs = sems.shape[0]
    rows = out.shape[0] // runs
    copies = []
    for i in range(runs):
        run = pl.ds(i * rows, rows)
        copies.append(pltpu.make_async_copy(feats.at[run], out.at[run], sems.at[i]))
    for copy in copies:
        copy.start()
    for copy in copies:
        copy.wait()


def tail_kernel(first, count, feats, out, held, sem):
    rows = out.shape[0]
    copy = pltpu.make_async_copy(feats.at[pl.ds(first, rows)], held, sem)
    copy.start()
    copy.wait()
    row = lax.broadcasted_iota(jnp.int32, held.shape, 0) + first
    out[...] = jnp.where(row < count[0:1, :], held[...], jnp.zeros_like(held))


def split(node_feats, count):
    rows, width = node_feats.shape
    half = (rows // 2, width)
    out = pltpu.VMEM(half, node_feats.dtype)
    options = dict(
        out_shape=out,
        out_specs=ON_CHIP,
        compiler_params=PARAMS,
        cost_estimate=COST,
    )
    node_feats = in_hbm(node_feats)
    head = pl.pallas_call(
        head_kernel,
        in_specs=[OFF_CHIP],
        scratch_shapes=[pltpu.SemaphoreType.DMA((2,))],
        name="head_of_slab",
        **options,
    )(node_feats)
    tail = pl.pallas_call(
        functools.partial(tail_kernel, rows // 2),
        in_specs=[ON_CHIP, OFF_CHIP],
        scratch_shapes=[out, pltpu.SemaphoreType.DMA],
        name="tail_of_slab",
        **options,
    )(in_vmem(count), node_feats)
    return [head, tail]


def thirds_kernel(head, tail, *outs):
    at, cut = 0, head.shape[0]
    for out in outs:
        end = at + out.shape[0]
        middle = min(max(cut, at), end)
        if middle > at:
            out[: middle - at] = head[at:middle]
        if end > middle:
            out[middle - at :] = tail[middle - cut : end - cut]
        at = end


def thirds(slab, size):
    rows, width = sum(piece.shape[0] for piece in slab), slab[0].shape[1]
    less = rows // 3 // size * size
    outs = [
        pltpu.VMEM((count, width), slab[0].dtype)
        for count in (rows - 2 * less, less, less)
    ]
    return pl.pallas_call(
        thirds_kernel,
        out_shape=outs,
        in_specs=[ON_CHIP] * 2,
        out_specs=[ON_CHIP] * 3,
        compiler_params=PARAMS,
        cost_estimate=COST,
        name="thirds",
    )(*map(in_vmem, slab))


def place_slab(slab, panels, size):
    at = 0
    for piece in slab:
        rows = piece.shape[0]
        panels[at : at + rows, :] = piece[...]
        at += rows
    panels[at:, :] = jnp.zeros((size, panels.shape[1]), panels.dtype)


def offset_of(step, spans):
    sign = 2 * lax.axis_index("rep") - 1
    return spans // 2 + sign * (0, 1, -1, -2, 2)[step]


def table_kernel(columns, out, sem):
    copy = pltpu.make_async_copy(columns, out, sem)
    copy.start()
    copy.wait()


def table_of(columns):
    return pl.pallas_call(
        table_kernel,
        out_shape=pltpu.SMEM(columns.shape, columns.dtype),
        in_specs=[pl.BlockSpec(memory_space=pl.ANY)],
        out_specs=SCALARS,
        scratch_shapes=[pltpu.SemaphoreType.DMA],
        compiler_params=PARAMS,
        cost_estimate=COST,
        name="table",
    )(columns)


def terms(panels, table, first, slots, tiles, at):
    size = tiles.shape[-1]
    rhs = []
    for k in range(slots):
        rows = pl.ds(pl.multiple_of(table[first + k] * size, size), size)
        rhs.append(panels[rows, :])
    return [tiles[at, k] for k in range(slots)], rhs


def multiplied(lhs, rhs):
    return jnp.dot(
        jnp.concatenate(lhs, axis=1),
        jnp.concatenate(rhs, axis=0),
        preferred_element_type=jnp.float32,
    )


def halves(groups):
    rep = lax.axis_index("rep")
    return (1 - rep) * (groups // 2), rep * (groups // 2)


def product_kernel(step, fetched, ahead, parts, halved, pieces, spans, table, *refs):
    refs = list(refs)
    slab = [refs.pop(0) for _ in range(pieces)]
    held = refs.pop(0) if fetched else None
    total = refs.pop(0) if fetched else None
    tiles = refs.pop(0) if ahead or parts or not fetched else None
    outs = [refs.pop(0) for _ in range(2 if halved else 1)]
    later = [refs.pop(0) for _ in ahead]
    part_refs = [[refs.pop(0) for _ in range(runs)] for _, _, runs in parts]
    panels, sems = refs.pop(0), refs.pop(0)
    if not fetched:
        held = refs.pop(0)
    groups, slots, size, _ = held.shape
    copies = []
    if not fetched:
        copies.append((tiles.at[:, 0, offset_of(step, spans)], held))
    now = len(copies)
    for other, target in zip(ahead, later):
        copies.append((tiles.at[:, 0, offset_of(other, spans)], target))
    for (other, half, _), targets in zip(parts, part_refs):
        for i, target in enumerate(targets):
            count = target.shape[0]
            run = pl.ds(halves(groups)[half] + i * count, count)
            copies.append((tiles.at[run, 0, offset_of(other, spans)], target))
    copies = [
        pltpu.make_async_copy(source, target, sems.at[i])
        for i, (source, target) in enumerate(copies)
    ]
    for copy in copies:
        copy.start()
    place_slab(slab, panels, size)
    for copy in copies[:now]:
        copy.wait()
    first = offset_of(step, spans) * (groups * slots)
    for out, start in zip(outs, halves(groups) if halved else (0,)):
        for i in range(out.shape[0]):
            g = start + i
            value = multiplied(*terms(panels, table, first + g * slots, slots, held, g))
            if fetched:
                value = value + total[g]
            out[i] = value.astype(out.dtype)
    for copy in copies[now:]:
        copy.wait()


def product(
    step, table, slab, tiles, held=None, total=None, ahead=(), parts=(), halved=False
):
    groups, _, spans, slots, size, _ = tiles.shape
    rows, width = sum(piece.shape[0] for piece in slab), slab[0].shape[1]
    fetched = held is not None
    shape = (groups, slots, size, size)
    operands = [in_smem(table), *map(in_vmem, slab)]
    specs = [SCALARS] + [ON_CHIP] * len(slab)
    if fetched:
        operands += [in_vmem(held), in_vmem(total)]
        specs += [ON_CHIP] * 2
    if ahead or parts or not fetched:
        operands.append(in_hbm(tiles))
        specs.append(OFF_CHIP)
    panels = pltpu.VMEM((rows + size, width), slab[0].dtype)
    count = groups // 2 if halved else groups
    out_shape = [pltpu.VMEM((count, size, width), jnp.float32)] * (groups // count)
    out_shape += [pltpu.VMEM(shape, tiles.dtype)] * len(ahead)
    for _, _, runs in parts:
        run = (groups // 2 // runs, *shape[1:])
        out_shape += [pltpu.VMEM(run, tiles.dtype)] * runs
    later = len(ahead) + sum(runs for _, _, runs in parts)
    scratch = [panels, pltpu.SemaphoreType.DMA((1 + later,))]
    if not fetched:
        scratch.append(pltpu.VMEM(shape, tiles.dtype))
    outs = pl.pallas_call(
        functools.partial(
            product_kernel, step, fetched, ahead, parts, halved, len(slab), spans
        ),
        out_shape=out_shape,
        in_specs=specs,
        out_specs=[ON_CHIP] * len(out_shape),
        scratch_shapes=scratch,
        compiler_params=PARAMS,
        cost_estimate=COST,
        name="product",
    )(*operands)
    return outs if len(outs) > 1 else outs[0]


def half_kernel(half, pieces, works, spans, *refs):
    refs = list(refs)
    tables = [refs.pop(0) for _ in works]
    slab = [refs.pop(0) for _ in range(pieces or 1)]
    tiles = [[refs.pop(0) for _ in range(count)] for _, count in works]
    total, out = refs.pop(0), refs.pop(0)
    groups, size, _ = out.shape
    panels = slab[0]
    if pieces:
        panels = refs.pop(0)
        place_slab(slab, panels, size)
    start = halves(2 * groups)[half]
    for g in range(groups):
        lhs, rhs = [], []
        for table, (step, count), runs in zip(tables, works, tiles):
            slots, run = runs[0].shape[1], groups // count
            first = (offset_of(step, spans) * (2 * groups) + start + g) * slots
            more = terms(panels, table, first, slots, runs[g // run], g % run)
            lhs, rhs = lhs + more[0], rhs + more[1]
        out[g] = (total[g] + multiplied(lhs, rhs)).astype(out.dtype)


def half_product(half, slab, works, total, spans, dtype=jnp.float32, placed=None):
    _, size, width = total.shape
    rows = sum(piece.shape[0] for piece in slab) + (0 if placed else size)
    tables = [in_smem(table) for _, table, _ in works]
    vmem = [*slab, *(runs for _, _, tiles in works for runs in tiles), total]
    out_shape = [pltpu.VMEM(total.shape, dtype)]
    panels, scratch = pltpu.VMEM((rows, width), slab[0].dtype), []
    if placed is None:
        scratch.append(panels)
    elif not placed:
        out_shape.append(panels)
    outs = pl.pallas_call(
        functools.partial(
            half_kernel,
            half,
            0 if placed else len(slab),
            [(step, len(tiles)) for step, _, tiles in works],
            spans,
        ),
        out_shape=out_shape,
        in_specs=[SCALARS] * len(tables) + [ON_CHIP] * len(vmem),
        out_specs=[ON_CHIP] * len(out_shape),
        scratch_shapes=scratch,
        compiler_params=PARAMS,
        cost_estimate=COST,
        name="half_product",
    )(*tables, *map(in_vmem, vmem))
    return outs if len(outs) > 1 else outs[0]


def add_kernel(kept, got, out):
    out[...] = (kept[...] + got[...].astype(jnp.float32)).astype(out.dtype)


def add(kept, got):
    return pl.pallas_call(
        add_kernel,
        out_shape=pltpu.VMEM(got.shape, got.dtype),
        in_specs=[ON_CHIP, ON_CHIP],
        out_specs=ON_CHIP,
        compiler_params=PARAMS,
        name="add_halves",
    )(in_vmem(kept), in_vmem(got))


def finish_kernel(other, count, agg, weight, bias, *refs):
    out, held, sems = refs[-3:]
    copies = []
    groups, size, _ = agg.shape
    feat = lax.axis_index("feat")
    feat = 1 - feat if other else feat
    live = count[0:1, :] - (lax.axis_index("rep") * (2 * groups) + feat) * size
    biased = bias[...].astype(jnp.float32)
    row = lax.broadcasted_iota(jnp.int32, held.shape[1:], 0)
    for g in range(groups):
        value = jnp.dot(agg[g], weight[...], preferred_element_type=jnp.float32)
        value = jnp.maximum(value + biased, 0.0)
        held[g] = jnp.where(row + 2 * g * size < live, value, 0.0).astype(out.dtype)
        if (g + 1) % (groups // 2) == 0:
            run = pl.ds(g + 1 - groups // 2, groups // 2)
            source, target = held.at[run], out.at[run, feat]
            copies.append(pltpu.make_async_copy(source, target, sems.at[len(copies)]))
            copies[-1].start()
    for copy in copies:
        copy.wait()


def finish(count, agg, weight, bias, out=None):
    groups, size, _ = agg.shape
    share = weight.shape[1]
    before = [] if out is None else [out]
    return pl.pallas_call(
        functools.partial(finish_kernel, out is not None),
        out_shape=jax.ShapeDtypeStruct((groups, 2, size, share), agg.dtype),
        in_specs=[ON_CHIP] * 4 + [OFF_CHIP] * len(before),
        out_specs=OFF_CHIP,
        scratch_shapes=[
            pltpu.VMEM((groups, size, share), agg.dtype),
            pltpu.SemaphoreType.DMA((2,)),
        ],
        input_output_aliases={4: 0} if before else {},
        compiler_params=PARAMS,
        name="finish",
    )(in_vmem(count), in_vmem(agg), in_vmem(weight), in_vmem(bias), *before)


def local(node_feats, tile_vals, tile_cols, tile_count, node_count, weight, bias):
    size = tile_vals.shape[-1]
    groups, _, spans, slots = tile_vals.shape[:4]
    reach = spans // 2
    rep, feat = lax.axis_index("rep"), lax.axis_index("feat")
    panels = node_feats.shape[0] // size
    slot_ids = rep * slots + jnp.arange(slots, dtype=jnp.int32)
    live = slot_ids[None, None, :] < tile_count[:, 0, :, None]
    columns = jnp.where(live, tile_cols[:, 0], panels)
    columns = columns.transpose(1, 0, 2).reshape(-1).astype(jnp.int32)
    share = weight.shape[1] // lax.axis_size("feat")
    weight_own = lax.dynamic_slice_in_dim(weight, feat * share, share, 1)
    bias_own = lax.dynamic_slice_in_dim(bias, feat * share, share, 0)[None]

    count = jnp.broadcast_to(node_count[None], (8, node_feats.shape[1]))
    own = split(node_feats, count)
    near = [along_ring(piece) for piece in own]
    table = table_of(columns)
    total, near_tiles, *gifts = product(
        OWN,
        table,
        own,
        tile_vals,
        ahead=(NEAR,),
        parts=((FAR_OTHER, GIVEN, GIFTS),),
    )
    gifts = [between_cores(gift) for gift in gifts]
    other_columns = between_cores(columns)
    first, (total, near_tiles) = after(near[0], (total, near_tiles))
    near = [first, near[1]]
    far = [further_along(piece) for piece in near]
    near_other = [between_cores(piece) for piece in thirds(near, size)]
    near_tiles, (gifts, other_columns) = after(near_tiles, (gifts, other_columns))
    total, near_other_tiles, far_given_tiles, far_kept_tiles, far_other_tiles = product(
        NEAR,
        table,
        near,
        tile_vals,
        near_tiles,
        total,
        ahead=(NEAR_OTHER,),
        parts=((FAR, GIVEN, 1), (FAR, KEPT, 1), (FAR_OTHER, KEPT, 1)),
    )
    total, other_table = after(total, table_of(other_columns))
    totals = product(
        NEAR_OTHER, table, near_other, tile_vals, near_other_tiles, total, halved=True
    )
    first, totals = after(far[0], totals)
    far = [first, far[1]]
    far_other = [between_cores(piece) for piece in far]
    given, far_panels = half_product(
        GIVEN,
        far,
        [(FAR, table, [far_given_tiles])],
        totals[0],
        spans,
        jnp.bfloat16,
        placed=False,
    )
    got = between_cores(given)
    works = [(FAR, table, [far_kept_tiles]), (FAR, other_table, gifts)]
    kept = half_product(KEPT, [far_panels], works, totals[1], spans, placed=True)
    works = [(FAR_OTHER, table, [far_other_tiles])]
    kept = half_product(KEPT, far_other, works, kept, spans)
    mine = add(kept, got)
    theirs = between_feats(mine)
    out = finish(count, mine, weight_own, bias_own)
    out = finish(count, theirs, weight_own, bias_own, out)
    return out.reshape(-1, share)


def solution(mesh):
    return jax.shard_map(
        local,
        mesh=mesh,
        in_specs=(
            P("team", None),
            P("team", "feat", None, "rep", None, None),
            P("team", "feat", None, "rep"),
            P("team", "feat", None),
            P("team"),
            P(),
            P(),
        ),
        out_specs=P(("team", "rep"), "feat"),
        check_vma=False,
    )
```
